512 devices in a mesh: rows: 32 (over y, x, core), cols: 16 (over z).
Axes of the slice: x: 4, y: 4, z: 16, core: 2. Of those that a mesh axis runs over, the one named last changes fastest.
Arguments:
- encoded: bfloat16 [1024, 512, 384], P('rows', 'cols'), may hold values from -6 to 6
- conv_weight: bfloat16 [3, 3, 384, 384], replicated, may hold values from -0.109375 to 0.109375
- film_table: bfloat16 [360, 2, 384], replicated, may hold values from -3 to 3
- lead: int32 [1], replicated, may hold values from 0 to 359
Outputs:
- updated: bfloat16 [1024, 512, 384], P('rows', 'cols')
The draws below stay inside these ranges and needn't reach their ends.
All inputs are finite; a program needn't handle non-finite values.
Results may differ from the reference program's by a relative error of at most 0.006.
Values may be sent and summed in bfloat16 or wider, within the bound.
A program may use at most 64 MiB of HBM per device.

```python
import jax
import jax.numpy as jnp
from jax import lax

HID = 384
LEADS = 360
DILATION_RATE = 128
NROWS = 1024
NCOLS = 512


def block_levels(stream_key, extent, shards, smallest, high):
    def one(axis_at, shards_of):
        heights = jax.random.uniform(jax.random.fold_in(jax.random.fold_in(stream_key, 6), axis_at), (shards_of,), jnp.float32, smallest / len(shards), high / len(shards))
        return jnp.repeat(jnp.exp(heights), extent[axis_at] // shards_of).reshape((-1,) + (1,) * (len(extent) - axis_at - 1))

    loudness = one(*shards[0])
    for cut in shards[1:]:
        loudness = loudness * one(*cut)
    return loudness


def normal_values(rng, shape, width, most, shards=(), held_as=jnp.bfloat16):
    array = jax.random.normal(rng, shape, jnp.float32) * width
    if len(shards) > 0:
        array = block_levels(rng, shape, shards, -0.22, 0.18) * array
    return jnp.clip(array, min=-most, max=most).astype(held_as)


def setup_inputs(seed: int = 0) -> dict:
    arg_keys = jax.random.split(jax.random.key(seed), 5)
    return {
        "encoded": normal_values(arg_keys[0], (NROWS, NCOLS, HID), 1.0, 6.0, ((0, 32), (1, 16))),
        "conv_weight": normal_values(arg_keys[1], (3, 3, HID, HID), (9 * HID) ** -0.5, 0.109375),
        "film_table": normal_values(arg_keys[2], (LEADS, 2, HID), 0.5, 3.0),
        "lead": jax.random.randint(arg_keys[3], (1,), 0, LEADS).astype(jnp.int32),
    }


def reference(encoded, conv_weight, film_table, lead):
    active = jnp.maximum(encoded, jnp.zeros((), jnp.bfloat16))
    conv = lax.conv_general_dilated(
        active.astype(jnp.float32)[None],
        conv_weight.astype(jnp.float32),
        (1, 1),
        [(DILATION_RATE, DILATION_RATE), (DILATION_RATE, DILATION_RATE)],
        rhs_dilation=(DILATION_RATE, DILATION_RATE),
        dimension_numbers=("NHWC", "HWIO", "NHWC"),
        precision=lax.Precision.HIGHEST,
    )[0]
    selected_taps = film_table[lead[0]].astype(jnp.float32)
    updated = encoded.astype(jnp.float32) + conv * (1.0 + selected_taps[0]) + selected_taps[1]
    return updated.astype(jnp.bfloat16)
```

```python
import functools

import jax
import jax.numpy as jnp
from jax import lax
from jax.experimental import pallas as pl
from jax.experimental.pallas import tpu as pltpu
from jax.sharding import PartitionSpec as P

DILATION_RATE = 128
CHUNKS = 8
AHEAD = 2
CELLS = 16
MESH = pl.DeviceIdType.MESH


def kernel(dims, lead, enc_hbm, w_hbm, film_hbm, out_hbm, enc, w, film, mid, left, right, done,
           load_sem, own_sem, in_send, in_recv, col_send, col_recv, out_send, out_recv):
    n_rows, n_cols, row_step, col_step = dims
    per = enc.shape[0] // n_rows
    take = per // CHUNKS
    row, col = lax.axis_index("rows"), lax.axis_index("cols")
    me, lane = row // row_step, row % row_step
    has_left, has_right = col >= col_step, col < (n_cols - 1) * col_step

    def peer(step):
        other = lax.rem(me + step, n_rows)
        return other, (other * row_step + lane, col)

    def source(step):
        return lax.rem(me + n_rows - step, n_rows)

    loads = [
        pltpu.make_async_copy(enc_hbm, enc, load_sem.at[0]),
        pltpu.make_async_copy(w_hbm, w, load_sem.at[1]),
        pltpu.make_async_copy(film_hbm, film, load_sem.at[2]),
    ]
    for load in loads:
        load.start()

    barrier = pltpu.get_barrier_semaphore()

    def greet(step, carry):
        pl.semaphore_signal(barrier, inc=1, device_id=peer(step)[1], device_id_type=MESH)
        return carry

    @pl.when(has_left)
    def _():
        pl.semaphore_signal(barrier, inc=1, device_id=(row, col - col_step), device_id_type=MESH)

    @pl.when(has_right)
    def _():
        pl.semaphore_signal(barrier, inc=1, device_id=(row, col + col_step), device_id_type=MESH)

    lax.fori_loop(1, n_rows, greet, 0)

    for buffer in (mid, left, right):
        zero = jnp.zeros(buffer.shape[:1] + buffer.shape[2:], buffer.dtype)
        buffer[:, 0] = zero
        buffer[:, n_rows + 1] = zero

    @pl.when(jnp.logical_not(has_left))
    def _():
        left[...] = jnp.zeros_like(left)

    @pl.when(jnp.logical_not(has_right))
    def _():
        right[...] = jnp.zeros_like(right)

    loads[0].wait()
    greeted = n_rows - 1 + has_left.astype(jnp.int32) + has_right.astype(jnp.int32)
    pl.semaphore_wait(barrier, greeted)

    def own_copy(part):
        return pltpu.make_async_copy(
            enc.at[pl.ds(me * per + part * take, take)], mid.at[part, me + 1], own_sem.at[part])

    def in_copy(part, step):
        other, device = peer(step)
        return pltpu.make_async_remote_copy(
            src_ref=enc.at[pl.ds(other * per + part * take, take)],
            dst_ref=mid.at[part, me + 1],
            send_sem=in_send.at[part, step],
            recv_sem=in_recv.at[part, step],
            device_id=device, device_id_type=MESH)

    def in_arrival(part, step):
        return pltpu.make_async_remote_copy(
            src_ref=enc.at[pl.ds(0, take)],
            dst_ref=mid.at[part, source(step) + 1],
            send_sem=in_send.at[part, step],
            recv_sem=in_recv.at[part, step],
            device_id=peer(step)[1], device_id_type=MESH)

    def col_copy(part, way):
        buffer, shift = ((left, col_step), (right, -col_step))[way]
        return pltpu.make_async_remote_copy(
            src_ref=mid.at[part, pl.ds(1, n_rows)],
            dst_ref=buffer.at[part, pl.ds(1, n_rows)],
            send_sem=col_send.at[part, way],
            recv_sem=col_recv.at[part, way],
            device_id=(row, col + shift), device_id_type=MESH)

    def out_copy(part, step):
        other, device = peer(step)
        return pltpu.make_async_remote_copy(
            src_ref=done.at[part, other],
            dst_ref=out_hbm.at[pl.ds(me * per + part * take, take)],
            send_sem=out_send.at[part, step],
            recv_sem=out_recv.at[part, step],
            device_id=device, device_id_type=MESH)

    def out_arrival(part, step):
        return pltpu.make_async_remote_copy(
            src_ref=done.at[part, 0],
            dst_ref=out_hbm.at[pl.ds(source(step) * per + part * take, take)],
            send_sem=out_send.at[part, step],
            recv_sem=out_recv.at[part, step],
            device_id=peer(step)[1], device_id_type=MESH)

    def out_own(part):
        return pltpu.make_async_copy(
            done.at[part, me], out_hbm.at[pl.ds(me * per + part * take, take)], own_sem.at[CHUNKS + part])

    def each(first, last, act):
        def body(step, carry):
            act(step)
            return carry
        lax.fori_loop(first, last, body, 0)

    def spread(part):
        own_copy(part).start()
        each(1, n_rows, lambda step: in_copy(part, step).start())

    def send_columns(part):
        @pl.when(has_right)
        def _():
            col_copy(part, 0).start()

        @pl.when(has_left)
        def _():
            col_copy(part, 1).start()

    def columns_sent(part):
        @pl.when(has_right)
        def _():
            col_copy(part, 0).wait_send()

        @pl.when(has_left)
        def _():
            col_copy(part, 1).wait_send()

    def columns_arrived(part):
        @pl.when(has_left)
        def _():
            col_copy(part, 0).wait_recv()

        @pl.when(has_right)
        def _():
            col_copy(part, 1).wait_recv()

    chans = enc.shape[-1]
    cells = n_rows * take * CELLS

    def compute(part):
        picked = film[lead[0]].astype(jnp.float32)
        gamma, beta = picked[0:1], picked[1:2]
        total = jnp.zeros((cells, chans), jnp.float32)
        for kx, buffer in enumerate((left, mid, right)):
            for ky in range(3):
                block = jnp.maximum(buffer[part, pl.ds(ky, n_rows)], 0).reshape(cells, chans)
                total += jnp.dot(block, w[ky, kx], preferred_element_type=jnp.float32)
        here = mid[part, pl.ds(1, n_rows)].reshape(cells, chans).astype(jnp.float32)
        updated = here + total * (1.0 + gamma) + beta
        done[part] = updated.astype(jnp.bfloat16).reshape(done.shape[1:])

    each(0, 2, spread)

    def stage(part, carry):
        @pl.when(part < CHUNKS)
        def _():
            own_copy(part).wait()
            each(1, n_rows, lambda step: in_arrival(part, step).wait_recv())

            @pl.when(part >= AHEAD)
            def _():
                columns_sent(part - AHEAD)

            send_columns(part)

            @pl.when(part + 2 < CHUNKS)
            def _():
                spread(part + 2)

        @pl.when(part == 0)
        def _():
            loads[1].wait()
            loads[2].wait()

        @pl.when(part >= AHEAD)
        def _():
            ready = part - AHEAD
            columns_arrived(ready)
            compute(ready)
            out_own(ready).start()
            each(1, n_rows, lambda step: out_copy(ready, step).start())

        return carry

    lax.fori_loop(0, CHUNKS + AHEAD, stage, 0)

    def finish(part):
        @pl.when(part >= CHUNKS - AHEAD)
        def _():
            columns_sent(part)

        out_own(part).wait()

        def one(step):
            in_copy(part, step).wait_send()
            out_copy(part, step).wait_send()
            out_arrival(part, step).wait_recv()

        each(1, n_rows, one)

    each(0, CHUNKS, finish)


def local(encoded, conv_weight, film_table, lead):
    height, width, chans = encoded.shape
    row_step, col_step = DILATION_RATE // height, DILATION_RATE // width
    n_rows = lax.axis_size("rows") // row_step
    n_cols = lax.axis_size("cols") // col_step
    units = height * width // CELLS
    take = units // n_rows // CHUNKS
    padded = (CHUNKS, n_rows + 2, take, CELLS, chans)
    hbm = pl.BlockSpec(memory_space=pltpu.HBM)
    dma = pltpu.SemaphoreType.DMA
    updated = pl.pallas_call(
        functools.partial(kernel, (n_rows, n_cols, row_step, col_step)),
        out_shape=jax.ShapeDtypeStruct((units, CELLS, chans), jnp.bfloat16),
        in_specs=[pl.BlockSpec(memory_space=pltpu.SMEM)] + [hbm] * 3,
        out_specs=pl.BlockSpec(memory_space=pl.ANY),
        scratch_shapes=[
            pltpu.VMEM((units, CELLS, chans), jnp.bfloat16),
            pltpu.VMEM(conv_weight.shape, jnp.bfloat16),
            pltpu.VMEM(film_table.shape, jnp.bfloat16),
            pltpu.VMEM(padded, jnp.bfloat16),
            pltpu.VMEM(padded, jnp.bfloat16),
            pltpu.VMEM(padded, jnp.bfloat16),
            pltpu.VMEM((CHUNKS, n_rows, take, CELLS, chans), jnp.bfloat16),
            dma((3,)),
            dma((2 * CHUNKS,)),
            dma((CHUNKS, n_rows)),
            dma((CHUNKS, n_rows)),
            dma((CHUNKS, 2)),
            dma((CHUNKS, 2)),
            dma((CHUNKS, n_rows)),
            dma((CHUNKS, n_rows)),
        ],
        compiler_params=pltpu.CompilerParams(
            collective_id=0, has_side_effects=True, vmem_limit_bytes=40 * 1024 * 1024),
        cost_estimate=pl.CostEstimate(
            flops=2 * 9 * height * width * chans * chans, bytes_accessed=5_000_000, transcendentals=0),
        name="dilated_block",
    )(lead, encoded.reshape(units, CELLS, chans), conv_weight, film_table)
    return updated.reshape(encoded.shape)


def solution(mesh):
    placed = (P("rows", "cols", None), P(), P(), P())
    return jax.shard_map(
        local, mesh=mesh, in_specs=placed, out_specs=P("rows", "cols", None), check_vma=False
    )
```

```python
import functools

import jax
import jax.numpy as jnp
from jax import lax
from jax.experimental import pallas as pl
from jax.experimental.pallas import tpu as pltpu
from jax.sharding import PartitionSpec as P

DILATION_RATE = 128
CHUNKS = 8
RAW = 3
LAG = 2
SETTLE = 2
CELLS = 16
VMEM_LIMIT = 40 * 1024 * 1024
MESH = pl.DeviceIdType.MESH


def kernel(dims, lead, enc_hbm, w_hbm, film_hbm, out, enc, w, film, mid, left, right, hop, raw, acc, done,
           load_sem, own_sem, in_send, in_recv, col_send, col_recv, raw_own, raw_send, raw_recv,
           out_send, out_recv):
    n_rows, n_cols, row_step, hops = dims
    per = enc.shape[1]
    take = per // CHUNKS
    chans = enc.shape[-1]
    cells = n_rows * take * CELLS
    row, col = lax.axis_index("rows"), lax.axis_index("cols")
    me, lane = row // row_step, row % row_step
    last_col = n_cols * hops - 1
    sides = (left, right)
    inside = pl.ds(1, n_rows)

    def peer(step):
        other = lax.rem(me + step, n_rows)
        return other, (other * row_step + lane, col)

    def source(step):
        return lax.rem(me + n_rows - step, n_rows)

    def each(first, last, act):
        def body(step, carry):
            act(step)
            return carry
        lax.fori_loop(first, last, body, 0)

    def holds(stage, way):
        if way == 0:
            return jnp.logical_and(col >= stage, col - stage <= last_col - hops)
        return jnp.logical_and(col + stage >= hops, col + stage <= last_col)

    loads = [
        pltpu.make_async_copy(enc_hbm, enc, load_sem.at[0]),
        pltpu.make_async_copy(w_hbm, w, load_sem.at[1]),
        pltpu.make_async_copy(film_hbm, film, load_sem.at[2]),
    ]
    for load in loads:
        load.start()

    barrier = pltpu.get_barrier_semaphore()
    below, above = col > 0, col < last_col

    @pl.when(below)
    def _():
        pl.semaphore_signal(barrier, inc=1, device_id=(row, col - 1), device_id_type=MESH)

    @pl.when(above)
    def _():
        pl.semaphore_signal(barrier, inc=1, device_id=(row, col + 1), device_id_type=MESH)

    each(1, n_rows, lambda step: pl.semaphore_signal(
        barrier, inc=1, device_id=peer(step)[1], device_id_type=MESH))

    for buffer in (mid, left, right):
        zero = jnp.zeros(buffer.shape[:1] + buffer.shape[2:], buffer.dtype)
        buffer[:, 0] = zero
        buffer[:, n_rows + 1] = zero

    for way in range(2):
        @pl.when(jnp.logical_not(holds(hops, way)))
        def _():
            sides[way][...] = jnp.zeros_like(sides[way])

    loads[0].wait()
    greeted = n_rows - 1 + below.astype(jnp.int32) + above.astype(jnp.int32)
    pl.semaphore_wait(barrier, greeted)

    def own_copy(part):
        return pltpu.make_async_copy(
            enc.at[me, pl.ds(part * take, take)], mid.at[part, me + 1], own_sem.at[part])

    def in_copy(part, step):
        other, device = peer(step)
        return pltpu.make_async_remote_copy(
            src_ref=enc.at[other, pl.ds(part * take, take)],
            dst_ref=mid.at[part, me + 1],
            send_sem=in_send.at[part],
            recv_sem=in_recv.at[part],
            device_id=device, device_id_type=MESH)

    others = pl.ds(0, n_rows - 1)

    def in_all(part):
        return pltpu.make_async_remote_copy(
            src_ref=mid.at[part, others], dst_ref=mid.at[part, others],
            send_sem=in_send.at[part], recv_sem=in_recv.at[part],
            device_id=peer(1)[1], device_id_type=MESH)

    def spread(part):
        own_copy(part).start()
        each(1, n_rows, lambda step: in_copy(part, step).start())

    def col_copy(part, stage, way, first=False, final=False):
        if stage > 0:
            src = hop.at[way, stage - 1, part]
        elif first:
            src = enc.at[:, pl.ds(part * take, take)]
        else:
            src = mid.at[part, inside]
        if stage < hops - 1:
            dst = hop.at[way, stage, part]
        elif final:
            dst = raw.at[way, part]
        else:
            dst = sides[way].at[part, inside]
        return pltpu.make_async_remote_copy(
            src_ref=src, dst_ref=dst,
            send_sem=col_send.at[way, stage, part],
            recv_sem=col_recv.at[way, stage, part],
            device_id=(row, col + (1, -1)[way]), device_id_type=MESH)

    def depart(part, first):
        for way in range(2):
            @pl.when(holds(0, way))
            def _():
                col_copy(part, 0, way, first=first).start()

    def relay(part, stage):
        for way in range(2):
            @pl.when(holds(stage, way))
            def _():
                col_copy(part, stage - 1, way).wait_recv()
                if stage < hops - 1:
                    col_copy(part, stage, way).start()
                else:
                    @pl.when(part < RAW)
                    def _():
                        col_copy(part, stage, way, final=True).start()

                    @pl.when(part >= RAW)
                    def _():
                        col_copy(part, stage, way).start()

    def land(part):
        for way in range(2):
            @pl.when(holds(hops, way))
            def _():
                col_copy(part, hops - 1, way).wait_recv()

    def raw_own_copy(part, way):
        return pltpu.make_async_copy(
            raw.at[way, part, me], sides[way].at[part, me + 1], raw_own.at[way, part])

    def raw_copy(part, way, step):
        other, device = peer(step)
        return pltpu.make_async_remote_copy(
            src_ref=raw.at[way, part, other],
            dst_ref=sides[way].at[part, me + 1],
            send_sem=raw_send.at[way, part],
            recv_sem=raw_recv.at[way, part],
            device_id=device, device_id_type=MESH)

    def raw_all(part, way):
        return pltpu.make_async_remote_copy(
            src_ref=raw.at[way, part, others], dst_ref=sides[way].at[part, others],
            send_sem=raw_send.at[way, part], recv_sem=raw_recv.at[way, part],
            device_id=peer(1)[1], device_id_type=MESH)

    def raw_spread(part):
        for way in range(2):
            @pl.when(holds(hops, way))
            def _():
                raw_own_copy(part, way).start()
                each(1, n_rows, lambda step: raw_copy(part, way, step).start())

    def raw_land(part):
        for way in range(2):
            @pl.when(holds(hops, way))
            def _():
                raw_own_copy(part, way).wait()
                raw_all(part, way).wait_recv()

    def out_copy(part, step):
        other, device = peer(step)
        return pltpu.make_async_remote_copy(
            src_ref=done.at[part, other],
            dst_ref=out.at[me, pl.ds(part * take, take)],
            send_sem=out_send.at[part],
            recv_sem=out_recv.at[part],
            device_id=device, device_id_type=MESH)

    def out_all(part):
        return pltpu.make_async_remote_copy(
            src_ref=done.at[part, others], dst_ref=done.at[part, others],
            send_sem=out_send.at[part], recv_sem=out_recv.at[part],
            device_id=peer(1)[1], device_id_type=MESH)

    def out_own(part):
        return pltpu.make_async_copy(
            done.at[part, me], out.at[me, pl.ds(part * take, take)], own_sem.at[CHUNKS + part])

    def taps(part, kx, buffer):
        total = None
        for ky in range(3):
            block = jnp.maximum(buffer[part, pl.ds(ky, n_rows)], 0).reshape(cells, chans)
            term = jnp.dot(block, w[ky, kx], preferred_element_type=jnp.float32)
            total = term if total is None else total + term
        return total

    def update(part):
        picked = film[lead[0]].astype(jnp.float32)
        gamma, beta = picked[0:1], picked[1:2]
        total = acc[part] + taps(part, 0, left) + taps(part, 2, right)
        here = mid[part, inside].reshape(cells, chans).astype(jnp.float32)
        updated = here + total * (1.0 + gamma) + beta
        done[part] = updated.astype(jnp.bfloat16).reshape(done.shape[1:])
        out_own(part).start()
        each(1, n_rows, lambda step: out_copy(part, step).start())

    def both(a, b):
        return jnp.logical_and(a, b)

    for part in range(RAW):
        depart(part, True)
    spread(RAW)
    spread(RAW + 1)
    for load in loads[1:]:
        load.wait()
    crossing = hops * LAG

    def round_(turn, carry):
        shared = both(turn >= RAW, turn < CHUNKS + RAW)
        arriving = lax.rem(turn, CHUNKS)

        @pl.when(shared)
        def _():
            own_copy(arriving).wait()
            in_all(arriving).wait_recv()

        @pl.when(both(shared, turn < CHUNKS))
        def _():
            depart(arriving, False)

        for stage in range(1, hops):
            part = turn - stage * LAG

            @pl.when(both(part >= 0, part < CHUNKS))
            def _():
                relay(part, stage)

        @pl.when(both(shared, turn + 2 < CHUNKS + RAW))
        def _():
            spread(lax.rem(turn + 2, CHUNKS))

        @pl.when(shared)
        def _():
            acc[arriving] = taps(arriving, 1, mid)
            in_all(arriving).wait_send()

        for stage in range(hops):
            sent = turn - stage * LAG - LAG

            @pl.when(both(sent >= 0, sent < CHUNKS))
            def _():
                for way in range(2):
                    @pl.when(holds(stage, way))
                    def _():
                        col_copy(sent, stage, way).wait_send()

        part = turn - crossing

        @pl.when(both(part >= 0, part < CHUNKS))
        def _():
            land(part)

        @pl.when(both(part >= 0, part < RAW))
        def _():
            raw_spread(part)

        def finished(late, carry):
            ready = part - late * SETTLE

            @pl.when(both(late == 1, both(ready >= 0, ready < RAW)))
            def _():
                raw_land(ready)
                for way in range(2):
                    @pl.when(holds(hops, way))
                    def _():
                        raw_all(ready, way).wait_send()

            @pl.when(both(ready >= RAW * (1 - late), ready < jnp.where(late == 1, RAW, CHUNKS)))
            def _():
                update(ready)

            return carry

        lax.fori_loop(0, 2, finished, 0)
        return carry

    lax.fori_loop(0, CHUNKS + crossing, round_, 0)

    def finish(part):
        out_own(part).wait()
        out_all(part).wait_send()
        out_all(part).wait_recv()

    each(0, CHUNKS, finish)


def local(encoded, conv_weight, film_table, lead):
    height, width, chans = encoded.shape
    row_step, hops = DILATION_RATE // height, DILATION_RATE // width
    n_rows = lax.axis_size("rows") // row_step
    n_cols = lax.axis_size("cols") // hops
    per = height * width // CELLS // n_rows
    take = per // CHUNKS
    piece = (take, CELLS, chans)
    bf16, dma = jnp.bfloat16, pltpu.SemaphoreType.DMA
    hbm = pl.BlockSpec(memory_space=pltpu.HBM)
    operands = (encoded.reshape(n_rows, per, CELLS, chans), conv_weight, film_table)
    updated = pl.pallas_call(
        functools.partial(kernel, (n_rows, n_cols, row_step, hops)),
        out_shape=pltpu.VMEM((n_rows, per, CELLS, chans), bf16),
        in_specs=[pl.BlockSpec(memory_space=pltpu.SMEM)] + [hbm] * 3,
        out_specs=pl.BlockSpec(memory_space=pltpu.VMEM),
        scratch_shapes=[
            pltpu.VMEM((n_rows, per, CELLS, chans), bf16),
            pltpu.VMEM(conv_weight.shape, bf16),
            pltpu.VMEM(film_table.shape, bf16),
            pltpu.VMEM((CHUNKS, n_rows + 2) + piece, bf16),
            pltpu.VMEM((CHUNKS, n_rows + 2) + piece, bf16),
            pltpu.VMEM((CHUNKS, n_rows + 2) + piece, bf16),
            pltpu.VMEM((2, hops - 1, CHUNKS, n_rows) + piece, bf16),
            pltpu.VMEM((2, RAW, n_rows) + piece, bf16),
            pltpu.VMEM((CHUNKS, n_rows * take * CELLS, chans), jnp.float32),
            pltpu.VMEM((CHUNKS, n_rows) + piece, bf16),
            dma((3,)),
            dma((2 * CHUNKS,)),
            dma((CHUNKS,)),
            dma((CHUNKS,)),
            dma((2, hops, CHUNKS)),
            dma((2, hops, CHUNKS)),
            dma((2, RAW)),
            dma((2, RAW)),
            dma((2, RAW)),
            dma((CHUNKS,)),
            dma((CHUNKS,)),
        ],
        compiler_params=pltpu.CompilerParams(
            collective_id=0, has_side_effects=True, vmem_limit_bytes=VMEM_LIMIT),
        cost_estimate=pl.CostEstimate(
            flops=2 * 9 * height * width * chans * chans, bytes_accessed=5_000_000, transcendentals=0),
        name="dilated_block",
    )(lead, *(pltpu.with_memory_space_constraint(a, pltpu.HBM) for a in operands))
    return updated.reshape(encoded.shape)


def solution(mesh):
    placed = (P("rows", "cols", None), P(), P(), P())
    return jax.shard_map(
        local, mesh=mesh, in_specs=placed, out_specs=P("rows", "cols", None), check_vma=False
    )
```

```python
import functools

import jax
import jax.numpy as jnp
from jax import lax
from jax.experimental import pallas as pl
from jax.experimental.pallas import tpu as pltpu
from jax.sharding import PartitionSpec as P

DILATION_RATE = 128
CHUNKS = 8
FIRST = 3
LAG = 2
SETTLE = 3
VMEM_LIMIT = 40 * 1024 * 1024
MESH = pl.DeviceIdType.MESH


def kernel(dims, lead, enc_hbm, w_hbm, film_hbm, out, enc, w, film, sides, hop, rows, sums, acc,
           load_sem, col_send, col_recv, row_send, row_recv):
    row_step, hops, last_row, last_col = dims
    row, col = lax.axis_index("rows"), lax.axis_index("cols")

    def both(a, b):
        return jnp.logical_and(a, b)

    def holds(stage, way):
        if way == 0:
            return both(col >= stage, col - stage <= last_col - hops)
        return both(col + stage >= hops, col + stage <= last_col)

    gives = (row <= last_row - row_step, row >= row_step)
    takes = (row >= row_step, row <= last_row - row_step)

    def row_device(way):
        return (row + (row_step, -row_step)[way], col)

    def col_device(way):
        return (row, col + (1, -1)[way])

    loads = [
        pltpu.make_async_copy(enc_hbm, enc, load_sem.at[0]),
        pltpu.make_async_copy(w_hbm, w, load_sem.at[1]),
        pltpu.make_async_copy(film_hbm, film, load_sem.at[2]),
    ]
    for load in loads:
        load.start()

    barrier = pltpu.get_barrier_semaphore()
    greeted = jnp.int32(0)
    for near, device in (
        (col < last_col, col_device(0)), (col > 0, col_device(1)),
        (gives[0], row_device(0)), (gives[1], row_device(1)),
    ):
        @pl.when(near)
        def _():
            pl.semaphore_signal(barrier, inc=1, device_id=device, device_id_type=MESH)

        greeted += near.astype(jnp.int32)

    for way in range(2):
        @pl.when(jnp.logical_not(holds(hops, way)))
        def _():
            sides[way] = jnp.zeros(sides.shape[1:], sides.dtype)

        @pl.when(jnp.logical_not(takes[way]))
        def _():
            rows[way] = jnp.zeros(rows.shape[1:], rows.dtype)

    loads[0].wait()
    pl.semaphore_wait(barrier, greeted)

    def col_copy(part, stage, way, first=False):
        if stage > 0:
            src = hop.at[way, stage - 1, part]
        else:
            src = enc.at[part] if first else sums.at[way, part]
        dst = hop.at[way, stage, part] if stage < hops - 1 else sides.at[way, part]
        return pltpu.make_async_remote_copy(
            src_ref=src, dst_ref=dst,
            send_sem=col_send.at[way, stage, part],
            recv_sem=col_recv.at[way, stage, part],
            device_id=col_device(way), device_id_type=MESH)

    def row_copy(part, way, first=False):
        return pltpu.make_async_remote_copy(
            src_ref=sums.at[way, part] if first else enc.at[part],
            dst_ref=rows.at[way, part],
            send_sem=row_send.at[way, part],
            recv_sem=row_recv.at[way, part],
            device_id=row_device(way), device_id_type=MESH)

    def depart(part, first):
        for way in range(2):
            @pl.when(holds(0, way))
            def _():
                col_copy(part, 0, way, first).start()

    def relay(part, stage):
        for way in range(2):
            @pl.when(holds(stage, way))
            def _():
                col_copy(part, stage - 1, way).wait_recv()
                col_copy(part, stage, way).start()

    def land(part):
        for way in range(2):
            @pl.when(holds(hops, way))
            def _():
                col_copy(part, hops - 1, way).wait_recv()

    def send_rows(part, first):
        for way in range(2):
            @pl.when(gives[way])
            def _():
                row_copy(part, way, first).start()

    def rows_arrived(part):
        for way in range(2):
            @pl.when(takes[way])
            def _():
                row_copy(part, way).wait_recv()

    def rows_sent(part):
        for way in range(2):
            @pl.when(gives[way])
            def _():
                row_copy(part, way).wait_send()

    def active(ref):
        return jnp.maximum(ref[...], 0)

    def tap(block, ky, kx):
        return jnp.dot(block, w[ky, kx], preferred_element_type=jnp.float32)

    def update(part, ends):
        picked = film[lead[0]].astype(jnp.float32)
        gamma, beta = picked[0:1], picked[1:2]
        conv = acc[part, 1] + ends[0, part].astype(jnp.float32) + ends[1, part].astype(jnp.float32)
        out[part] = (enc[part].astype(jnp.float32) + conv * (1.0 + gamma) + beta).astype(jnp.bfloat16)

    def begin_first(part):
        block = active(enc.at[part])
        for ky in range(3):
            acc[part, ky] = tap(block, ky, 1)

    def end_first(part):
        left, right = active(sides.at[0, part]), active(sides.at[1, part])
        for way, ky in ((0, 0), (1, 2)):
            total = acc[part, ky] + tap(left, ky, 0) + tap(right, ky, 2)
            sums[way, part] = total.astype(jnp.bfloat16)
        send_rows(part, True)
        acc[part, 1] += tap(left, 1, 0) + tap(right, 1, 2)

    def prepare(part):
        rows_arrived(part)
        blocks = (active(rows.at[0, part]), active(enc.at[part]), active(rows.at[1, part]))

        def across(kx):
            return tap(blocks[0], 0, kx) + tap(blocks[1], 1, kx) + tap(blocks[2], 2, kx)

        sums[0, part] = across(0).astype(jnp.bfloat16)
        sums[1, part] = across(2).astype(jnp.bfloat16)
        acc[part, 1] = across(1)
        rows_sent(part)

    depart(0, True)
    send_rows(FIRST, False)
    send_rows(FIRST + 1, False)
    for load in loads[1:]:
        load.wait()
    crossing = hops * LAG

    def round_(turn, carry):
        @pl.when(both(turn > 0, turn < FIRST))
        def _():
            depart(turn, True)

        @pl.when(both(turn >= FIRST, turn < CHUNKS))
        def _():
            depart(turn, False)

        for stage in range(1, hops):
            part = turn - stage * LAG

            @pl.when(both(part >= 0, part < CHUNKS))
            def _():
                relay(part, stage)

        @pl.when(both(turn > 0, turn + FIRST + 1 < CHUNKS))
        def _():
            send_rows(turn + FIRST + 1, False)

        @pl.when(turn < FIRST)
        def _():
            begin_first(turn)

        @pl.when(both(turn + 1 >= FIRST, turn + 1 < CHUNKS))
        def _():
            prepare(turn + 1)

        for stage in range(hops):
            sent = turn - stage * LAG - LAG

            @pl.when(both(sent >= 0, sent < CHUNKS))
            def _():
                for way in range(2):
                    @pl.when(holds(stage, way))
                    def _():
                        col_copy(sent, stage, way).wait_send()

        part = turn - crossing

        @pl.when(both(part >= 0, part < CHUNKS))
        def _():
            land(part)

        @pl.when(both(part >= 0, part < FIRST))
        def _():
            end_first(part)

        @pl.when(both(part >= FIRST, part < CHUNKS))
        def _():
            update(part, sides)

        settled = part - SETTLE

        @pl.when(both(settled >= 0, settled < FIRST))
        def _():
            rows_arrived(settled)
            update(settled, rows)
            rows_sent(settled)

        return carry

    lax.fori_loop(0, max(CHUNKS, FIRST + SETTLE) + crossing, round_, 0)


def local(encoded, conv_weight, film_table, lead):
    height, width, chans = encoded.shape
    row_step, hops = DILATION_RATE // height, DILATION_RATE // width
    last_row, last_col = lax.axis_size("rows") - 1, lax.axis_size("cols") - 1
    piece = (height * width // CHUNKS, chans)
    bf16, dma = jnp.bfloat16, pltpu.SemaphoreType.DMA
    hbm = pl.BlockSpec(memory_space=pltpu.HBM)
    operands = (encoded.reshape((CHUNKS,) + piece), conv_weight, film_table)
    updated = pl.pallas_call(
        functools.partial(kernel, (row_step, hops, last_row, last_col)),
        out_shape=pltpu.VMEM((CHUNKS,) + piece, bf16),
        in_specs=[pl.BlockSpec(memory_space=pltpu.SMEM)] + [hbm] * 3,
        out_specs=pl.BlockSpec(memory_space=pltpu.VMEM),
        scratch_shapes=[
            pltpu.VMEM((CHUNKS,) + piece, bf16),
            pltpu.VMEM(conv_weight.shape, bf16),
            pltpu.VMEM(film_table.shape, bf16),
            pltpu.VMEM((2, CHUNKS) + piece, bf16),
            pltpu.VMEM((2, hops - 1, CHUNKS) + piece, bf16),
            pltpu.VMEM((2, CHUNKS) + piece, bf16),
            pltpu.VMEM((2, CHUNKS) + piece, bf16),
            pltpu.VMEM((CHUNKS, 3) + piece, jnp.float32),
            dma((3,)),
            dma((2, hops, CHUNKS)),
            dma((2, hops, CHUNKS)),
            dma((2, CHUNKS)),
            dma((2, CHUNKS)),
        ],
        compiler_params=pltpu.CompilerParams(
            collective_id=0, has_side_effects=True, vmem_limit_bytes=VMEM_LIMIT),
        cost_estimate=pl.CostEstimate(
            flops=2 * 9 * height * width * chans * chans, bytes_accessed=5_000_000, transcendentals=0),
        name="dilated_block",
    )(lead, *(pltpu.with_memory_space_constraint(a, pltpu.HBM) for a in operands))
    return updated.reshape(encoded.shape)


def solution(mesh):
    placed = (P("rows", "cols", None), P(), P(), P())
    return jax.shard_map(
        local, mesh=mesh, in_specs=placed, out_specs=P("rows", "cols", None), check_vma=False
    )
```

```python
import functools

import jax
import jax.numpy as jnp
from jax import lax
from jax.experimental import pallas as pl
from jax.experimental.pallas import tpu as pltpu
from jax.sharding import PartitionSpec as P

DILATION_RATE = 128
CHUNKS = 4
FIRST = 2
ROUNDS = (0, 1, 2, 3, 4)
KEEP = 1
SETTLE = 1
VMEM_LIMIT = 40 * 1024 * 1024
MESH = pl.DeviceIdType.MESH


def kernel(dims, lead, enc_hbm, w_hbm, film_hbm, out, enc, w, film, sides, hop, rows, sums, acc,
           load_sem, col_send, col_recv, row_send, row_recv):
    row_step, hops, last_row, last_col = dims
    row, col = lax.axis_index("rows"), lax.axis_index("cols")

    def both(a, b):
        return jnp.logical_and(a, b)

    def holds(stage, way):
        if way == 0:
            return both(col >= stage, col - stage <= last_col - hops)
        return both(col + stage >= hops, col + stage <= last_col)

    gives = (row <= last_row - row_step, row >= row_step)
    takes = (row >= row_step, row <= last_row - row_step)

    def row_device(way):
        return (row + (row_step, -row_step)[way], col)

    def col_device(way):
        return (row, col + (1, -1)[way])

    barrier = pltpu.get_barrier_semaphore()
    greeted = jnp.int32(0)
    for near, device in (
        (col < last_col, col_device(0)), (col > 0, col_device(1)),
        (gives[0], row_device(0)), (gives[1], row_device(1)),
    ):
        @pl.when(near)
        def _():
            pl.semaphore_signal(barrier, inc=1, device_id=device, device_id_type=MESH)

        greeted += near.astype(jnp.int32)

    loads = [
        pltpu.make_async_copy(enc_hbm, enc, load_sem.at[0]),
        pltpu.make_async_copy(w_hbm, w, load_sem.at[1]),
        pltpu.make_async_copy(film_hbm, film, load_sem.at[2]),
    ]
    for load in loads:
        load.start()

    loads[0].wait()
    pl.semaphore_wait(barrier, greeted)

    def col_copy(part, stage, way, first=False):
        if stage > 0:
            src = hop.at[way, stage - 1, part]
        else:
            src = enc.at[part] if first else sums.at[way, part]
        dst = hop.at[way, stage, part] if stage < hops - 1 else sides.at[way, part]
        return pltpu.make_async_remote_copy(
            src_ref=src, dst_ref=dst,
            send_sem=col_send.at[way, stage, part],
            recv_sem=col_recv.at[way, stage, part],
            device_id=col_device(way), device_id_type=MESH)

    def row_copy(part, way, first=False):
        return pltpu.make_async_remote_copy(
            src_ref=sums.at[way, part] if first else enc.at[part],
            dst_ref=rows.at[way, part],
            send_sem=row_send.at[way, part],
            recv_sem=row_recv.at[way, part],
            device_id=row_device(way), device_id_type=MESH)

    def depart(part, first):
        for way in range(2):
            @pl.when(holds(0, way))
            def _():
                col_copy(part, 0, way, first).start()

    def relay(part, stage):
        for way in range(2):
            @pl.when(holds(stage, way))
            def _():
                col_copy(part, stage - 1, way).wait_recv()
                col_copy(part, stage, way).start()

    def land(part):
        for way in range(2):
            @pl.when(holds(hops, way))
            def _():
                col_copy(part, hops - 1, way).wait_recv()

    def send_rows(part, first):
        for way in range(2):
            @pl.when(gives[way])
            def _():
                row_copy(part, way, first).start()

    def rows_arrived(part):
        for way in range(2):
            @pl.when(takes[way])
            def _():
                row_copy(part, way).wait_recv()

    def rows_sent(part):
        for way in range(2):
            @pl.when(gives[way])
            def _():
                row_copy(part, way).wait_send()

    def active(ref):
        return jnp.maximum(ref[...], 0)

    def tap(block, ky, kx):
        return jnp.dot(block, w[ky, kx], preferred_element_type=jnp.float32)

    def film_row(which):
        return film[lead[0]].astype(jnp.float32)[which:which + 1]

    def base(part, conv):
        acc[part, 1] = enc[part].astype(jnp.float32) + conv * (1.0 + film_row(0)) + film_row(1)

    def update(part, ends):
        late = ends[0, part].astype(jnp.float32) + ends[1, part].astype(jnp.float32)
        out[part] = (acc[part, 1] + late * (1.0 + film_row(0))).astype(jnp.bfloat16)

    def begin_first(part):
        block = active(enc.at[part])
        for ky in range(3):
            acc[part, ky] = tap(block, ky, 1)

    def end_first(part):
        left, right = active(sides.at[0, part]), active(sides.at[1, part])
        for way, ky in ((0, 0), (1, 2)):
            total = acc[part, ky] + tap(left, ky, 0) + tap(right, ky, 2)
            sums[way, part] = total.astype(jnp.bfloat16)
        send_rows(part, True)
        base(part, acc[part, 1] + tap(left, 1, 0) + tap(right, 1, 2))

    def prepare(part):
        rows_arrived(part)
        blocks = (active(rows.at[0, part]), active(enc.at[part]), active(rows.at[1, part]))

        def across(kx):
            return tap(blocks[0], 0, kx) + tap(blocks[1], 1, kx) + tap(blocks[2], 2, kx)

        sums[0, part] = across(0).astype(jnp.bfloat16)
        sums[1, part] = across(2).astype(jnp.bfloat16)
        base(part, across(1))
        rows_sent(part)

    depart(0, True)
    send_rows(FIRST, False)

    for way in range(2):
        @pl.when(jnp.logical_not(holds(hops, way)))
        def _():
            sides[way] = jnp.zeros(sides.shape[1:], sides.dtype)

        @pl.when(jnp.logical_not(takes[way]))
        def _():
            rows[way] = jnp.zeros(rows.shape[1:], rows.dtype)

    for load in loads[1:]:
        load.wait()
    crossing = ROUNDS[hops]

    def round_(turn, carry):
        @pl.when(both(turn > 0, turn < FIRST))
        def _():
            depart(turn, True)

        @pl.when(both(turn >= FIRST, turn < CHUNKS))
        def _():
            depart(turn, False)

        for stage in range(1, hops):
            part = turn - ROUNDS[stage]

            @pl.when(both(part >= 0, part < CHUNKS))
            def _():
                relay(part, stage)

        @pl.when(turn + FIRST + 1 < CHUNKS)
        def _():
            send_rows(turn + FIRST + 1, False)

        @pl.when(turn < FIRST)
        def _():
            begin_first(turn)

        @pl.when(both(turn + 1 >= FIRST, turn + 1 < CHUNKS))
        def _():
            prepare(turn + 1)

        for stage in range(hops):
            sent = turn - ROUNDS[stage] - KEEP

            @pl.when(both(sent >= 0, sent < CHUNKS))
            def _():
                for way in range(2):
                    @pl.when(holds(stage, way))
                    def _():
                        col_copy(sent, stage, way).wait_send()

        part = turn - crossing

        @pl.when(both(part >= 0, part < CHUNKS))
        def _():
            land(part)

        @pl.when(both(part >= 0, part < FIRST))
        def _():
            end_first(part)

        @pl.when(both(part >= FIRST, part < CHUNKS))
        def _():
            update(part, sides)

        settled = part - SETTLE

        @pl.when(both(settled >= 0, settled < FIRST))
        def _():
            rows_arrived(settled)
            update(settled, rows)
            rows_sent(settled)

        return carry

    lax.fori_loop(0, max(CHUNKS, FIRST + SETTLE) + crossing, round_, 0)


def local(encoded, conv_weight, film_table, lead):
    height, width, chans = encoded.shape
    row_step, hops = DILATION_RATE // height, DILATION_RATE // width
    last_row, last_col = lax.axis_size("rows") - 1, lax.axis_size("cols") - 1
    piece = (height * width // CHUNKS, chans)
    bf16, dma = jnp.bfloat16, pltpu.SemaphoreType.DMA
    hbm = pl.BlockSpec(memory_space=pltpu.HBM)
    operands = (encoded.reshape((CHUNKS,) + piece), conv_weight, film_table)
    updated = pl.pallas_call(
        functools.partial(kernel, (row_step, hops, last_row, last_col)),
        out_shape=pltpu.VMEM((CHUNKS,) + piece, bf16),
        in_specs=[pl.BlockSpec(memory_space=pltpu.SMEM)] + [hbm] * 3,
        out_specs=pl.BlockSpec(memory_space=pltpu.VMEM),
        scratch_shapes=[
            pltpu.VMEM((CHUNKS,) + piece, bf16),
            pltpu.VMEM(conv_weight.shape, bf16),
            pltpu.VMEM(film_table.shape, bf16),
            pltpu.VMEM((2, CHUNKS) + piece, bf16),
            pltpu.VMEM((2, hops - 1, CHUNKS) + piece, bf16),
            pltpu.VMEM((2, CHUNKS) + piece, bf16),
            pltpu.VMEM((2, CHUNKS) + piece, bf16),
            pltpu.VMEM((CHUNKS, 3) + piece, jnp.float32),
            dma((3,)),
            dma((2, hops, CHUNKS)),
            dma((2, hops, CHUNKS)),
            dma((2, CHUNKS)),
            dma((2, CHUNKS)),
        ],
        compiler_params=pltpu.CompilerParams(
            collective_id=0, has_side_effects=True, vmem_limit_bytes=VMEM_LIMIT),
        cost_estimate=pl.CostEstimate(
            flops=2 * 9 * height * width * chans * chans, bytes_accessed=5_000_000, transcendentals=0),
        name="dilated_block",
    )(lead, *(pltpu.with_memory_space_constraint(a, pltpu.HBM) for a in operands))
    return updated.reshape(encoded.shape)


def solution(mesh):
    placed = (P("rows", "cols", None), P(), P(), P())
    return jax.shard_map(
        local, mesh=mesh, in_specs=placed, out_specs=P("rows", "cols", None), check_vma=False
    )
```

```python
import functools

import jax
import jax.numpy as jnp
from jax import lax
from jax.experimental import pallas as pl
from jax.experimental.pallas import tpu as pltpu
from jax.sharding import PartitionSpec as P

DILATION_RATE = 128
CHUNKS = 4
FIRST = 2
ROUNDS = (0, 1, 2, 3, 4)
KEEP = 1
SETTLE = 1
VMEM_LIMIT = 40 * 1024 * 1024
MESH = pl.DeviceIdType.MESH


def kernel(dims, lead, enc_hbm, w_hbm, film_hbm, out, enc, w, film, sides, hop, rows, sums, acc,
           load_sem, col_send, col_recv, row_send, row_recv, vouch_sem, open_sem):
    row_step, hops, last_row, last_col = dims
    row, col = lax.axis_index("rows"), lax.axis_index("cols")

    def both(a, b):
        return jnp.logical_and(a, b)

    def holds(stage, way):
        if way == 0:
            return both(col >= stage, col - stage <= last_col - hops)
        return both(col + stage >= hops, col + stage <= last_col)

    gives = (row <= last_row - row_step, row >= row_step)
    takes = (row >= row_step, row <= last_row - row_step)

    def row_device(way):
        return (row + (row_step, -row_step)[way], col)

    def col_device(way):
        return (row, col + (1, -1)[way])

    place = lax.rem(col, hops)
    broker = both(place > 0, place < hops - 1)
    client = (row, col + jnp.where(place < hops // 2, -1, 1))
    barrier = pltpu.get_barrier_semaphore()
    greeted = jnp.int32(0)
    for near, device in (
        (col < last_col, col_device(0)), (col > 0, col_device(1)),
        (both(broker, gives[0]), row_device(0)), (both(broker, gives[1]), row_device(1)),
    ):
        @pl.when(near)
        def _():
            pl.semaphore_signal(barrier, inc=1, device_id=device, device_id_type=MESH)

        greeted += near.astype(jnp.int32)

    loads = [
        pltpu.make_async_copy(enc_hbm, enc, load_sem.at[0]),
        pltpu.make_async_copy(w_hbm, w, load_sem.at[1]),
        pltpu.make_async_copy(film_hbm, film, load_sem.at[2]),
    ]
    for load in loads:
        load.start()

    loads[0].wait()
    pl.semaphore_wait(barrier, greeted)

    def col_copy(part, stage, way, first=False):
        if stage > 0:
            src = hop.at[way, stage - 1, part]
        else:
            src = enc.at[part] if first else sums.at[way, part]
        dst = hop.at[way, stage, part] if stage < hops - 1 else sides.at[way, part]
        return pltpu.make_async_remote_copy(
            src_ref=src, dst_ref=dst,
            send_sem=col_send.at[way, stage, part],
            recv_sem=col_recv.at[way, stage, part],
            device_id=col_device(way), device_id_type=MESH)

    def row_copy(part, way, first=False):
        return pltpu.make_async_remote_copy(
            src_ref=sums.at[way, part] if first else enc.at[part],
            dst_ref=rows.at[way, part],
            send_sem=row_send.at[way, part],
            recv_sem=row_recv.at[way, part],
            device_id=row_device(way), device_id_type=MESH)

    def depart(part, first):
        for way in range(2):
            @pl.when(holds(0, way))
            def _():
                col_copy(part, 0, way, first).start()

    def relay(part, stage):
        for way in range(2):
            @pl.when(holds(stage, way))
            def _():
                col_copy(part, stage - 1, way).wait_recv()
                col_copy(part, stage, way).start()

    def left_behind(part, stage):
        for way in range(2):
            @pl.when(holds(stage, way))
            def _():
                col_copy(part, stage, way).wait_send()

    def land(part):
        for way in range(2):
            @pl.when(holds(hops, way))
            def _():
                col_copy(part, hops - 1, way).wait_recv()

    def send_rows(part, first):
        for way in range(2):
            @pl.when(gives[way])
            def _():
                row_copy(part, way, first).start()

    def rows_arrived(part):
        for way in range(2):
            @pl.when(takes[way])
            def _():
                row_copy(part, way).wait_recv()

    def rows_sent(part):
        for way in range(2):
            @pl.when(gives[way])
            def _():
                row_copy(part, way).wait_send()

    def active(ref):
        return jnp.maximum(ref[...], 0)

    def tap(block, ky, kx):
        return jnp.dot(block, w[ky, kx], preferred_element_type=jnp.float32)

    def film_row(which):
        return film[lead[0]].astype(jnp.float32)[which:which + 1]

    def base(part, conv):
        acc[part, 1] = enc[part].astype(jnp.float32) + conv * (1.0 + film_row(0)) + film_row(1)

    def update(part, ends):
        late = ends[0, part].astype(jnp.float32) + ends[1, part].astype(jnp.float32)
        out[part] = (acc[part, 1] + late * (1.0 + film_row(0))).astype(jnp.bfloat16)

    def begin_first(part):
        block = active(enc.at[part])
        for ky in range(3):
            acc[part, ky] = tap(block, ky, 1)

    def end_first(part):
        left, right = active(sides.at[0, part]), active(sides.at[1, part])
        for way, ky in ((0, 0), (1, 2)):
            total = acc[part, ky] + tap(left, ky, 0) + tap(right, ky, 2)
            sums[way, part] = total.astype(jnp.bfloat16)
        send_rows(part, True)
        base(part, acc[part, 1] + tap(left, 1, 0) + tap(right, 1, 2))

    def prepare(part):
        rows_arrived(part)
        blocks = (active(rows.at[0, part]), active(enc.at[part]), active(rows.at[1, part]))

        def across(kx):
            return tap(blocks[0], 0, kx) + tap(blocks[1], 1, kx) + tap(blocks[2], 2, kx)

        sums[0, part] = across(0).astype(jnp.bfloat16)
        sums[1, part] = across(2).astype(jnp.bfloat16)
        base(part, across(1))
        rows_sent(part)

    for part in range(FIRST):
        depart(part, True)

    for way in range(2):
        @pl.when(jnp.logical_not(holds(hops, way)))
        def _():
            sides[way] = jnp.zeros(sides.shape[1:], sides.dtype)

        @pl.when(jnp.logical_not(takes[way]))
        def _():
            rows[way] = jnp.zeros(rows.shape[1:], rows.dtype)

    for load in loads[1:]:
        load.wait()
    for part in range(FIRST):
        begin_first(part)

    @pl.when(broker)
    def _():
        for way in range(2):
            @pl.when(gives[way])
            def _():
                pl.semaphore_signal(vouch_sem, inc=1, device_id=row_device(way), device_id_type=MESH)

        pl.semaphore_wait(vouch_sem, takes[0].astype(jnp.int32) + takes[1].astype(jnp.int32))
        pl.semaphore_signal(open_sem, inc=1, device_id=client, device_id_type=MESH)

    @pl.when(jnp.logical_not(broker))
    def _():
        pl.semaphore_wait(open_sem, 1)

    send_rows(FIRST, False)
    crossing = ROUNDS[hops]

    for turn in range(1, max(CHUNKS, FIRST + SETTLE) + crossing):
        for stage in range(1, hops):
            part = turn - ROUNDS[stage]
            if 0 <= part < FIRST:
                relay(part, stage)

        if FIRST <= turn < CHUNKS:
            prepare(turn)
            depart(turn, False)
            if turn + 1 < CHUNKS:
                send_rows(turn + 1, False)

        for stage in range(1, hops):
            part = turn - ROUNDS[stage]
            if FIRST <= part < CHUNKS:
                relay(part, stage)

        for stage in range(hops):
            sent = turn - ROUNDS[stage] - KEEP
            if 0 <= sent < CHUNKS:
                left_behind(sent, stage)

        part = turn - crossing
        if 0 <= part < CHUNKS:
            land(part)
            if part < FIRST:
                end_first(part)
            else:
                update(part, sides)

        settled = part - SETTLE
        if 0 <= settled < FIRST:
            rows_arrived(settled)
            update(settled, rows)
            rows_sent(settled)


def local(encoded, conv_weight, film_table, lead):
    height, width, chans = encoded.shape
    row_step, hops = DILATION_RATE // height, DILATION_RATE // width
    last_row, last_col = lax.axis_size("rows") - 1, lax.axis_size("cols") - 1
    piece = (height * width // CHUNKS, chans)
    bf16, dma = jnp.bfloat16, pltpu.SemaphoreType.DMA
    hbm = pl.BlockSpec(memory_space=pltpu.HBM)
    operands = (encoded.reshape((CHUNKS,) + piece), conv_weight, film_table)
    updated = pl.pallas_call(
        functools.partial(kernel, (row_step, hops, last_row, last_col)),
        out_shape=pltpu.VMEM((CHUNKS,) + piece, bf16),
        in_specs=[pl.BlockSpec(memory_space=pltpu.SMEM)] + [hbm] * 3,
        out_specs=pl.BlockSpec(memory_space=pltpu.VMEM),
        scratch_shapes=[
            pltpu.VMEM((CHUNKS,) + piece, bf16),
            pltpu.VMEM(conv_weight.shape, bf16),
            pltpu.VMEM(film_table.shape, bf16),
            pltpu.VMEM((2, CHUNKS) + piece, bf16),
            pltpu.VMEM((2, hops - 1, CHUNKS) + piece, bf16),
            pltpu.VMEM((2, CHUNKS) + piece, bf16),
            pltpu.VMEM((2, CHUNKS) + piece, bf16),
            pltpu.VMEM((CHUNKS, 3) + piece, jnp.float32),
            dma((3,)),
            dma((2, hops, CHUNKS)),
            dma((2, hops, CHUNKS)),
            dma((2, CHUNKS)),
            dma((2, CHUNKS)),
            pltpu.SemaphoreType.REGULAR,
            pltpu.SemaphoreType.REGULAR,
        ],
        compiler_params=pltpu.CompilerParams(
            collective_id=0, has_side_effects=True, vmem_limit_bytes=VMEM_LIMIT),
        cost_estimate=pl.CostEstimate(
            flops=2 * 9 * height * width * chans * chans, bytes_accessed=5_000_000, transcendentals=0),
        name="dilated_block",
    )(lead, *(pltpu.with_memory_space_constraint(a, pltpu.HBM) for a in operands))
    return updated.reshape(encoded.shape)


def solution(mesh):
    placed = (P("rows", "cols", None), P(), P(), P())
    return jax.shard_map(
        local, mesh=mesh, in_specs=placed, out_specs=P("rows", "cols", None), check_vma=False
    )
```

```python
import functools

import jax
import jax.numpy as jnp
from jax import lax
from jax.experimental import pallas as pl
from jax.experimental.pallas import tpu as pltpu
from jax.sharding import PartitionSpec as P

DILATION_RATE = 128
CHUNKS = 4
FIRST = 2
ROUNDS = (0, 1, 2, 3, 4)
KEEP = 1
SETTLE = 1
VMEM_LIMIT = 40 * 1024 * 1024
MESH = pl.DeviceIdType.MESH


def kernel(dims, lead, enc_hbm, w_hbm, film_hbm, out, enc, w, film, sides, hop, rows, sums, acc,
           load_sem, col_send, col_recv, row_send, row_recv, vouch_sem, open_sem):
    row_step, hops, last_row, last_col = dims
    row, col = lax.axis_index("rows"), lax.axis_index("cols")

    def both(a, b):
        return jnp.logical_and(a, b)

    def holds(stage, way):
        if way == 0:
            return both(col >= stage, col - stage <= last_col - hops)
        return both(col + stage >= hops, col + stage <= last_col)

    gives = (row <= last_row - row_step, row >= row_step)
    takes = (row >= row_step, row <= last_row - row_step)

    def row_device(way):
        return (row + (row_step, -row_step)[way], col)

    def col_device(way):
        return (row, col + (1, -1)[way])

    place = lax.rem(col, hops)
    broker = both(place > 0, place < hops - 1)
    client = (row, col + jnp.where(place < hops // 2, -1, 1))
    barrier = pltpu.get_barrier_semaphore()
    greeted = jnp.int32(0)
    for near, device in (
        (col < last_col, col_device(0)), (col > 0, col_device(1)),
        (both(broker, gives[0]), row_device(0)), (both(broker, gives[1]), row_device(1)),
    ):
        @pl.when(near)
        def _():
            pl.semaphore_signal(barrier, inc=1, device_id=device, device_id_type=MESH)

        greeted += near.astype(jnp.int32)

    loads = [
        pltpu.make_async_copy(enc_hbm, enc, load_sem.at[0]),
        pltpu.make_async_copy(w_hbm, w, load_sem.at[1]),
        pltpu.make_async_copy(film_hbm, film, load_sem.at[2]),
    ]
    for load in loads:
        load.start()

    loads[0].wait()
    pl.semaphore_wait(barrier, greeted)

    def col_copy(part, stage, way, first=False):
        if stage > 0:
            src = hop.at[way, stage - 1, part]
        else:
            src = enc.at[part] if first else sums.at[way, part]
        dst = hop.at[way, stage, part] if stage < hops - 1 else sides.at[way, part]
        return pltpu.make_async_remote_copy(
            src_ref=src, dst_ref=dst,
            send_sem=col_send.at[way, stage, part],
            recv_sem=col_recv.at[way, stage, part],
            device_id=col_device(way), device_id_type=MESH)

    def row_copy(part, way, first=False):
        return pltpu.make_async_remote_copy(
            src_ref=sums.at[way, part] if first else enc.at[part],
            dst_ref=rows.at[way, part],
            send_sem=row_send.at[way, part],
            recv_sem=row_recv.at[way, part],
            device_id=row_device(way), device_id_type=MESH)

    def depart(part, first):
        for way in range(2):
            @pl.when(holds(0, way))
            def _():
                col_copy(part, 0, way, first).start()

    def relay(part, stage):
        for way in range(2):
            @pl.when(holds(stage, way))
            def _():
                col_copy(part, stage - 1, way).wait_recv()
                col_copy(part, stage, way).start()

    def left_behind(part, stage):
        for way in range(2):
            @pl.when(holds(stage, way))
            def _():
                col_copy(part, stage, way).wait_send()

    def land(part, ways):
        for way in ways:
            @pl.when(holds(hops, way))
            def _():
                col_copy(part, hops - 1, way).wait_recv()

    def send_rows(part, first):
        for way in range(2):
            @pl.when(gives[way])
            def _():
                row_copy(part, way, first).start()

    def rows_arrived(part):
        for way in range(2):
            @pl.when(takes[way])
            def _():
                row_copy(part, way).wait_recv()

    def rows_sent(part):
        for way in range(2):
            @pl.when(gives[way])
            def _():
                row_copy(part, way).wait_send()

    def active(ref):
        return jnp.maximum(ref[...], 0)

    def tap(block, ky, kx):
        return jnp.dot(block, w[ky, kx], preferred_element_type=jnp.float32)

    def film_row(which):
        return film[lead[0]].astype(jnp.float32)[which:which + 1]

    def base(part, conv):
        acc[part, 1] = enc[part].astype(jnp.float32) + conv * (1.0 + film_row(0)) + film_row(1)

    def update(part, ends):
        late = ends[0, part].astype(jnp.float32) + ends[1, part].astype(jnp.float32)
        out[part] = (acc[part, 1] + late * (1.0 + film_row(0))).astype(jnp.bfloat16)

    def begin_first(part):
        block = active(enc.at[part])
        for ky in range(3):
            acc[part, ky] = tap(block, ky, 1)

    def end_first(part):
        left, right = active(sides.at[0, part]), active(sides.at[1, part])
        for way, ky in ((0, 0), (1, 2)):
            total = acc[part, ky] + tap(left, ky, 0) + tap(right, ky, 2)
            sums[way, part] = total.astype(jnp.bfloat16)
        send_rows(part, True)
        base(part, acc[part, 1] + tap(left, 1, 0) + tap(right, 1, 2))

    def prepare(part):
        rows_arrived(part)
        blocks = (active(rows.at[0, part]), active(enc.at[part]), active(rows.at[1, part]))

        def across(kx):
            return tap(blocks[0], 0, kx) + tap(blocks[1], 1, kx) + tap(blocks[2], 2, kx)

        sums[0, part] = across(0).astype(jnp.bfloat16)
        sums[1, part] = across(2).astype(jnp.bfloat16)
        base(part, across(1))
        rows_sent(part)

    for part in range(FIRST):
        depart(part, True)

    for way in range(2):
        @pl.when(jnp.logical_not(holds(hops, way)))
        def _():
            sides[way] = jnp.zeros(sides.shape[1:], sides.dtype)

        @pl.when(jnp.logical_not(takes[way]))
        def _():
            rows[way] = jnp.zeros(rows.shape[1:], rows.dtype)

    for load in loads[1:]:
        load.wait()
    @pl.when(broker)
    def _():
        for way in range(2):
            @pl.when(gives[way])
            def _():
                pl.semaphore_signal(vouch_sem, inc=1, device_id=row_device(way), device_id_type=MESH)

        pl.semaphore_wait(vouch_sem, takes[0].astype(jnp.int32) + takes[1].astype(jnp.int32))
        pl.semaphore_signal(open_sem, inc=1, device_id=client, device_id_type=MESH)

    @pl.when(jnp.logical_not(broker))
    def _():
        pl.semaphore_wait(open_sem, 1)

    send_rows(FIRST, False)
    for part in range(FIRST):
        begin_first(part)

    crossing = ROUNDS[hops]

    for turn in range(1, max(CHUNKS, FIRST + SETTLE) + crossing):
        for stage in range(1, hops):
            part = turn - ROUNDS[stage]
            if 0 <= part < FIRST:
                relay(part, stage)

        if FIRST <= turn < CHUNKS:
            prepare(turn)
            depart(turn, False)
            if turn + 1 < CHUNKS:
                send_rows(turn + 1, False)

        for stage in range(1, hops):
            part = turn - ROUNDS[stage]
            if FIRST <= part < CHUNKS:
                relay(part, stage)

        for stage in range(hops):
            sent = turn - ROUNDS[stage] - KEEP
            if 0 <= sent < CHUNKS:
                left_behind(sent, stage)

        part = turn - crossing
        if 0 <= part < CHUNKS:
            if part < FIRST:
                land(part, (0, 1))
                end_first(part)
            else:
                land(part, (0,))
                acc[part, 1] += sides[0, part].astype(jnp.float32) * (1.0 + film_row(0))
                land(part, (1,))
                late = sides[1, part].astype(jnp.float32)
                out[part] = (acc[part, 1] + late * (1.0 + film_row(0))).astype(jnp.bfloat16)

        settled = part - SETTLE
        if 0 <= settled < FIRST:
            rows_arrived(settled)
            update(settled, rows)
            rows_sent(settled)


def local(encoded, conv_weight, film_table, lead):
    height, width, chans = encoded.shape
    row_step, hops = DILATION_RATE // height, DILATION_RATE // width
    last_row, last_col = lax.axis_size("rows") - 1, lax.axis_size("cols") - 1
    piece = (height * width // CHUNKS, chans)
    bf16, dma = jnp.bfloat16, pltpu.SemaphoreType.DMA
    hbm = pl.BlockSpec(memory_space=pltpu.HBM)
    operands = (encoded.reshape((CHUNKS,) + piece), conv_weight, film_table)
    updated = pl.pallas_call(
        functools.partial(kernel, (row_step, hops, last_row, last_col)),
        out_shape=pltpu.VMEM((CHUNKS,) + piece, bf16),
        in_specs=[pl.BlockSpec(memory_space=pltpu.SMEM)] + [hbm] * 3,
        out_specs=pl.BlockSpec(memory_space=pltpu.VMEM),
        scratch_shapes=[
            pltpu.VMEM((CHUNKS,) + piece, bf16),
            pltpu.VMEM(conv_weight.shape, bf16),
            pltpu.VMEM(film_table.shape, bf16),
            pltpu.VMEM((2, CHUNKS) + piece, bf16),
            pltpu.VMEM((2, hops - 1, CHUNKS) + piece, bf16),
            pltpu.VMEM((2, CHUNKS) + piece, bf16),
            pltpu.VMEM((2, CHUNKS) + piece, bf16),
            pltpu.VMEM((CHUNKS, 3) + piece, jnp.float32),
            dma((3,)),
            dma((2, hops, CHUNKS)),
            dma((2, hops, CHUNKS)),
            dma((2, CHUNKS)),
            dma((2, CHUNKS)),
            pltpu.SemaphoreType.REGULAR,
            pltpu.SemaphoreType.REGULAR,
        ],
        compiler_params=pltpu.CompilerParams(
            collective_id=0, has_side_effects=True, vmem_limit_bytes=VMEM_LIMIT),
        cost_estimate=pl.CostEstimate(
            flops=2 * 9 * height * width * chans * chans, bytes_accessed=5_000_000, transcendentals=0),
        name="dilated_block",
    )(lead, *(pltpu.with_memory_space_constraint(a, pltpu.HBM) for a in operands))
    return updated.reshape(encoded.shape)


def solution(mesh):
    placed = (P("rows", "cols", None), P(), P(), P())
    return jax.shard_map(
        local, mesh=mesh, in_specs=placed, out_specs=P("rows", "cols", None), check_vma=False
    )
```
